512 devices in a mesh: ctx: 64 (over y, z), ch: 8 (over x, core).
Axes of the slice: x: 4, y: 4, z: 16, core: 2. Of those that a mesh axis runs over, the one named last changes fastest.
Arguments:
- q_stream: bfloat16 [16384, 2048], P('ctx', 'ch'), may hold values from -6 to 6
- k_stream: bfloat16 [16384, 2048], P('ctx', 'ch'), may hold values from -6 to 6
- v_stream: bfloat16 [16384, 2048], P('ctx', 'ch'), may hold values from -6 to 6
- short_taps: float32 [3, 3, 2048], P(None, None, 'ch'), may hold values from -3 to 3
- short_bias: float32 [3, 2048], P(None, 'ch'), may hold values from -3 to 3
- long_filter: float32 [16384, 2048], P('ctx', 'ch'), may hold values from -0.046875 to 0.046875
- skip_gain: float32 [2048], P('ch'), may hold values from -4 to 4
- out_weight: bfloat16 [2048, 2048], P('ch'), may hold values from -0.1875 to 0.1875
- out_bias: float32 [2048], P('ch'), may hold values from -3 to 3
Outputs:
- mixed: bfloat16 [2048, 16384], P('ch', 'ctx')
The draws below stay inside these ranges and needn't reach their ends.
All inputs are finite; a program needn't handle non-finite values.
Results may differ from the reference program's by a relative error of at most 0.0049.
Values may be sent and summed in bfloat16 or wider, within the bound.
A program may use at most 64 MiB of HBM per device.

```python
import jax
import jax.numpy as jnp
from jax import lax

W = 2048
TOKENS = 16384


def with_spikes(values, stream_key, source, target, parts, factor):
    def block_of(position):
        return (jnp.arange(values.shape[position]) // (values.shape[position] // parts)).reshape((-1,) + (1,) * (values.ndim - 1 - position))

    one_side = jax.random.permutation(stream_key, parts)[block_of(target)]
    other_side = (block_of(target) + parts // 2) % parts
    return jnp.where((block_of(source) == one_side) | (block_of(source) == other_side), factor * values, values)


def shard_levels(own_key, dims, shards, smallest, top_value):
    def one(axis_at, blocks):
        draws = jax.random.uniform(jax.random.fold_in(jax.random.fold_in(own_key, 6), axis_at), (blocks,), jnp.float32, smallest / len(shards), top_value / len(shards))
        return jnp.repeat(jnp.exp(draws), dims[axis_at] // blocks).reshape((-1,) + (1,) * (len(dims) - axis_at - 1))

    level = one(*shards[0])
    for cut in shards[1:]:
        level = level * one(*cut)
    return level


def scatter_about(key, extent, width, bound, pieces=(), dtype=jnp.bfloat16):
    values = jax.random.normal(key, extent, jnp.float32) * width
    if len(pieces) > 0:
        values = shard_levels(key, extent, pieces, -0.22, 0.18) * values
    return jnp.clip(values, min=-bound, max=bound).astype(dtype)


def gaussian_with(own_key, dims, scale, limit, cuts, heavy, held_as=jnp.bfloat16):
    drawn = scale * jax.random.normal(own_key, dims, jnp.float32)
    if cuts:
        drawn = drawn * shard_levels(own_key, dims, cuts, -0.22, 0.18)
    return jnp.clip(with_spikes(drawn, jax.random.fold_in(own_key, 3), *heavy), -limit, limit).astype(held_as)


def setup_inputs(seed: int = 0) -> dict:
    seeds = jax.random.split(jax.random.key(seed), 10)
    q_stream = scatter_about(seeds[0], (TOKENS, W), 1.0, 6.0, ((0, 64), (1, 8)))
    k_stream = scatter_about(seeds[1], (TOKENS, W), 1.0, 6.0, ((0, 64), (1, 8)))
    v_stream = scatter_about(seeds[2], (TOKENS, W), 1.0, 6.0, ((0, 64), (1, 8)))
    short_taps = scatter_about(seeds[3], (3, 3, W), 0.6, 3.0, ((2, 8),), jnp.float32)
    short_bias = scatter_about(seeds[4], (3, W), 0.5, 3.0, ((1, 8),), jnp.float32)
    long_filter = scatter_about(seeds[5], (TOKENS, W), (1.0 / TOKENS ** 0.5), 0.046875, ((0, 64), (1, 8)), jnp.float32)
    skip_gain = scatter_about(seeds[6], (W,), 1.0, 4.0, ((0, 8),), jnp.float32)
    out_weight = gaussian_with(seeds[7], (W, W), W ** -0.5, 0.1875, ((0, 8),), (0, 1, 8, 2.0))
    out_bias = scatter_about(seeds[8], (W,), 0.5, 3.0, ((0, 8),), jnp.float32)
    return dict(q_stream=q_stream, k_stream=k_stream, v_stream=v_stream, short_taps=short_taps, short_bias=short_bias, long_filter=long_filter, skip_gain=skip_gain, out_weight=out_weight, out_bias=out_bias)


def short_conv(stream, tap_weights, offset):
    values = stream.astype(jnp.float32)
    tok_total = values.shape[0]
    padded = jnp.pad(values, ((2, 0), (0, 0)))
    return (tap_weights[0] * padded[:tok_total] + tap_weights[1] * padded[1:tok_total + 1]
            + tap_weights[2] * padded[2:] + offset)


def long_conv(gated, long_filter):
    tok_total, chan_total = gated.shape
    block_width = min(chan_total, 256)
    block_count = chan_total // block_width

    def per_block(operands):
        gated_block, filter_block = operands
        fft_length = 2 * tok_total
        spectrum = jnp.fft.rfft(gated_block, n=fft_length, axis=0) * jnp.fft.rfft(filter_block, n=fft_length, axis=0)
        return jnp.fft.irfft(spectrum, n=fft_length, axis=0)[:tok_total]

    gated_blocks = gated.reshape(tok_total, block_count, block_width).transpose(1, 0, 2)
    filter_blocks = long_filter.reshape(tok_total, block_count, block_width).transpose(1, 0, 2)
    result = lax.map(per_block, (gated_blocks, filter_blocks))
    return result.transpose(1, 0, 2).reshape(tok_total, chan_total)


def reference(q_stream, k_stream, v_stream, short_taps, short_bias, long_filter, skip_gain, out_weight, out_bias):
    short_q = short_conv(q_stream, short_taps[0], short_bias[0])
    short_k = short_conv(k_stream, short_taps[1], short_bias[1])
    short_v = short_conv(v_stream, short_taps[2], short_bias[2])
    gated = short_k * short_v
    convolved = long_conv(gated, long_filter)
    operator = (short_q * (convolved + skip_gain * gated)).astype(jnp.bfloat16)
    mixed = jnp.dot(out_weight.T, operator.T, preferred_element_type=jnp.float32) + out_bias[:, None]
    return mixed.astype(jnp.bfloat16)
```

```python
import functools

import jax
import jax.numpy as jnp
from jax import lax
from jax.experimental import pallas as pl
from jax.experimental.pallas import tpu as pltpu
from jax.sharding import PartitionSpec as P

MESH = pl.DeviceIdType.MESH
F32 = jnp.float32
BF16 = jnp.bfloat16
LANES = 128
STEP = 16


def remote(src, dst, send_sem, recv_sem, axis, target):
    return pltpu.make_async_remote_copy(
        src_ref=src, dst_ref=dst, send_sem=send_sem, recv_sem=recv_sem,
        device_id={axis: target}, device_id_type=MESH,
    )


def wait_bytes(ref, sem):
    pltpu.make_async_copy(ref, ref, sem).wait()


def kernel(
    ctx_n, ch_n,
    q_ref, k_ref, v_ref, taps_ref, sbias_ref, filt_ref, skip_ref, w_ref, obias_ref,
    out_ref,
    flat, halo_out, halo_in, wide, send_h, send_g, send_y, recv_h, recv_g, recv_y,
    gated_t, query_t, toeplitz, shifted, padded, acc, w_all, w_t, oper,
    send_sem, recv_sem, halo_sem, w_send, w_recv, o_send, o_recv,
):
    me = lax.axis_index("ctx")
    my_ch = lax.axis_index("ch")

    barrier = pltpu.get_barrier_semaphore()

    @pl.loop(1, ctx_n)
    def _(step):
        pl.semaphore_signal(
            barrier, inc=1, device_id={"ctx": lax.rem(me + step, ctx_n)}, device_id_type=MESH)

    @pl.loop(1, ch_n)
    def _(step):
        pl.semaphore_signal(
            barrier, inc=1, device_id={"ch": lax.rem(my_ch + step, ch_n)}, device_id_type=MESH)

    def pack(halves, dst):
        for half in range(2):
            flat[pl.ds(half, 256, stride=2), :] = halves[half]
        dst[...] = flat[...].reshape(ctx_n, 8, LANES).astype(BF16)

    def exchange(src, dst, which):
        @pl.loop(1, ctx_n)
        def _(step):
            target = lax.rem(me + step, ctx_n)
            remote(src.at[target], dst.at[me], send_sem.at[which], recv_sem.at[which],
                   "ctx", target).start()
        dst[me] = src[me]

    pack([filt_ref[pl.ds(half * LANES, LANES), :].T for half in range(2)], send_h)

    tails = [ref[240:256, :].astype(F32)[14:16] for ref in (q_ref, k_ref, v_ref)]
    halo_out[...] = jnp.concatenate(tails + [jnp.zeros((10, 256), F32)], axis=0).astype(BF16)
    for index, ref in enumerate((q_ref, k_ref, v_ref)):
        wide[index, pl.ds(8, 256), :] = ref[...].astype(F32)

    pl.semaphore_wait(barrier, ctx_n + ch_n - 2)

    ahead = lax.rem(me + 1, ctx_n)
    halo_copy = remote(halo_out, halo_in, halo_sem.at[0], halo_sem.at[1], "ctx", ahead)
    halo_copy.start()
    exchange(send_h, recv_h, 0)

    @pl.loop(1, ch_n)
    def _(step):
        target = lax.rem(my_ch + step, ch_n)
        remote(w_ref.at[:, pl.ds(pl.multiple_of(target * 256, 256), 256)], w_all.at[my_ch],
               w_send, w_recv, "ch", target).start()
    w_all[my_ch] = w_ref[:, pl.ds(pl.multiple_of(my_ch * 256, 256), 256)]

    halo_copy.wait()
    before = jnp.where(me > 0, halo_in[...].astype(F32), 0.0)
    for index in range(3):
        wide[index, 6:8, :] = before[2 * index:2 * index + 2, :]

    def short(index, half):
        at = half * LANES
        return (
            taps_ref[index, 0:1, :] * wide[index, pl.ds(6 + at, LANES), :]
            + taps_ref[index, 1:2, :] * wide[index, pl.ds(7 + at, LANES), :]
            + taps_ref[index, 2:3, :] * wide[index, pl.ds(8 + at, LANES), :]
            + sbias_ref[index:index + 1, :]
        )

    for half in range(2):
        gated_t[half] = (short(1, half) * short(2, half)).T
    pack([gated_t[0], gated_t[1]], send_g)
    exchange(send_g, recv_g, 1)

    for half in range(2):
        query_t[half] = short(0, half).T

    wait_bytes(recv_h.at[pl.ds(0, ctx_n - 1)], recv_sem.at[0])
    flat[...] = recv_h[...].astype(F32).reshape(512, LANES)
    keep = (lax.broadcasted_iota(jnp.int32, (LANES, LANES), 1)
            >= lax.broadcasted_iota(jnp.int32, (LANES, LANES), 0))

    @pl.loop(0, 4)
    def _(chan):
        def build(block, earlier):
            for half in range(2):
                row = flat[pl.ds(8 * block + 2 * chan + half, 1), :]
                rolled = pltpu.roll(
                    jnp.broadcast_to(row, (LANES, LANES)), 0, 1, stride=1, stride_axis=0)
                at = pl.multiple_of(256 * block + LANES * half, LANES)
                toeplitz[chan, pl.ds(at, LANES), :] = jnp.where(keep, rolled, earlier).astype(BF16)
                earlier = rolled
            return earlier
        lax.fori_loop(0, ctx_n, build, jnp.zeros((LANES, LANES), F32))

    wait_bytes(recv_g.at[pl.ds(0, ctx_n - 1)], recv_sem.at[1])
    flat[...] = recv_g[...].astype(F32).reshape(512, LANES)
    padded[0:STEP, :] = jnp.zeros((STEP, LANES), F32)

    @pl.loop(0, 4)
    def _(chan):
        for half in range(2):
            padded[pl.ds(STEP + half, 64, stride=2), :] = flat[
                pl.ds(2 * chan + half, 64, stride=8), :]
        for lag in range(STEP):
            shifted[:, pl.ds(lag * LANES, LANES)] = padded[
                pl.ds(STEP - lag, LANES), :].astype(BF16)
        for part in range(8):
            rows = LANES - STEP * part
            product = jnp.dot(
                shifted[0:rows, :], toeplitz[chan, pl.ds(2048 * part, 2048), :],
                preferred_element_type=F32)
            if part == 0:
                acc[...] = product
            else:
                acc[pl.ds(STEP * part, rows), :] += product
        for half in range(2):
            flat[pl.ds(2 * chan + half, 64, stride=8), :] = acc[pl.ds(half, 64, stride=2), :]

    send_y[...] = flat[...].reshape(ctx_n, 8, LANES).astype(BF16)
    exchange(send_y, recv_y, 2)

    wait_bytes(w_all.at[pl.ds(0, ch_n - 1)], w_recv)

    @pl.loop(0, ch_n)
    def _(index):
        w_t[index] = w_all[index].T
    skip_t = jnp.broadcast_to(skip_ref[...], (LANES, 256)).T
    bias_t = jnp.broadcast_to(obias_ref[...], (LANES, 256)).T

    wait_bytes(recv_y.at[pl.ds(0, ctx_n - 1)], recv_sem.at[2])
    flat[...] = recv_y[...].astype(F32).reshape(512, LANES)
    for half in range(2):
        conv = flat[pl.ds(half, 256, stride=2), :]
        oper[my_ch, :, half * LANES:(half + 1) * LANES] = (
            query_t[half] * (conv + skip_t * gated_t[half])).astype(BF16)

    @pl.loop(1, ch_n)
    def _(step):
        target = lax.rem(my_ch + step, ch_n)
        remote(oper.at[my_ch], oper.at[my_ch], o_send, o_recv.at[my_ch], "ch", target).start()

    total = jnp.dot(w_t[my_ch], oper[my_ch], preferred_element_type=F32)
    for step in range(1, ch_n):
        source = lax.rem(my_ch + step, ch_n)
        wait_bytes(oper.at[source], o_recv.at[source])
        total = total + jnp.dot(w_t[source], oper[source], preferred_element_type=F32)
    for half in range(2):
        cut = slice(half * LANES, (half + 1) * LANES)
        out_ref[:, cut] = (total[:, cut] + bias_t).astype(BF16)

    for which, ref in enumerate((send_h, send_g, send_y)):
        wait_bytes(ref.at[pl.ds(0, ctx_n - 1)], send_sem.at[which])
    wait_bytes(w_all.at[pl.ds(0, ch_n - 1)], w_send)
    wait_bytes(oper.at[pl.ds(0, ch_n - 1)], o_send)


def shards(q, k, v, taps, sbias, filt, skip, weight, obias):
    ctx_n, ch_n = lax.axis_size("ctx"), lax.axis_size("ch")
    vmem = pl.BlockSpec(memory_space=pltpu.VMEM)
    message = pltpu.VMEM((ctx_n, 8, LANES), BF16)
    dma = pltpu.SemaphoreType.DMA
    return pl.pallas_call(
        functools.partial(kernel, ctx_n, ch_n),
        out_shape=jax.ShapeDtypeStruct((256, 256), BF16),
        in_specs=[vmem] * 9,
        out_specs=vmem,
        scratch_shapes=[
            pltpu.VMEM((512, LANES), F32),
            pltpu.VMEM((16, 256), BF16),
            pltpu.VMEM((16, 256), BF16),
            pltpu.VMEM((3, 264, 256), F32),
            message, message, message, message, message, message,
            pltpu.VMEM((2, 256, LANES), F32),
            pltpu.VMEM((2, 256, LANES), F32),
            pltpu.VMEM((4, 16384, LANES), BF16),
            pltpu.VMEM((LANES, 2048), BF16),
            pltpu.VMEM((LANES + STEP, LANES), F32),
            pltpu.VMEM((LANES, LANES), F32),
            pltpu.VMEM((ch_n, 256, 256), BF16),
            pltpu.VMEM((ch_n, 256, 256), BF16),
            pltpu.VMEM((ch_n, 256, 256), BF16),
            dma((3,)), dma((3,)), dma((2,)), dma, dma, dma, dma((ch_n,)),
        ],
        compiler_params=pltpu.CompilerParams(
            collective_id=3, has_side_effects=True, vmem_limit_bytes=50 * 2**20),
    )(q, k, v, taps, sbias, filt, skip.reshape(1, -1), weight, obias.reshape(1, -1))


def solution(mesh):
    return jax.shard_map(
        shards,
        mesh=mesh,
        in_specs=(
            P("ctx", "ch"),
            P("ctx", "ch"),
            P("ctx", "ch"),
            P(None, None, "ch"),
            P(None, "ch"),
            P("ctx", "ch"),
            P("ch"),
            P("ch", None),
            P("ch"),
        ),
        out_specs=P("ch", "ctx"),
        check_vma=False,
    )
```

```python
import functools

import jax
import jax.numpy as jnp
from jax import lax
from jax.experimental import pallas as pl
from jax.experimental.pallas import tpu as pltpu
from jax.sharding import PartitionSpec as P

MESH = pl.DeviceIdType.MESH
F32 = jnp.float32
BF16 = jnp.bfloat16
LANES = 128
STEP = 16


def remote(src, dst, send_sem, recv_sem, axis, target):
    return pltpu.make_async_remote_copy(
        src_ref=src, dst_ref=dst, send_sem=send_sem, recv_sem=recv_sem,
        device_id={axis: target}, device_id_type=MESH,
    )


def wait_bytes(ref, sem):
    pltpu.make_async_copy(ref, ref, sem).wait()


def toeplitz_rows(recv_h, toeplitz, chunk, blocks):
    rows = lax.broadcasted_iota(jnp.int32, (STEP, LANES), 0)
    lanes = lax.broadcasted_iota(jnp.int32, (STEP, LANES), 1)
    keep = [(lanes >= rows) & (lanes < LANES - STEP * part) for part in range(8)]
    per_step = 4

    def build(index, earlier):
        earlier = list(earlier)
        bases = {}
        for inner in range(per_step):
            lags = recv_h[chunk, per_step * index + inner].astype(F32)
            for row in range(4):
                bases[inner, row] = pltpu.roll(
                    jnp.broadcast_to(lags[row:row + 1, :], (STEP, LANES)), 0, 1,
                    stride=1, stride_axis=0).astype(BF16)
        for inner in range(per_step):
            for row in range(4):
                chan, half = row // 2, row % 2
                base = bases[inner, row]
                at = pl.multiple_of(256 * (per_step * index + inner) + LANES * half, LANES)
                for part in range(8):
                    mixed = jnp.where(keep[part], base, earlier[chan])
                    if part:
                        mixed = pltpu.roll(mixed, STEP * part, 1)
                    toeplitz[2 * chunk + chan, pl.ds(at + STEP * part, STEP), :] = mixed
                earlier[chan] = base
        return tuple(earlier)

    zero = jnp.zeros((STEP, LANES), BF16)
    lax.fori_loop(0, blocks // per_step, build, (zero, zero))


def kernel(
    ctx_n, ch_n,
    q_ref, k_ref, v_ref, taps_ref, sbias_ref, filt_ref, skip_ref, w_ref, obias_ref,
    out_ref,
    flat, halo_out, halo_in, wide, send_h, send_g, send_y, recv_h, recv_g, recv_y,
    gated_t, query_t, toeplitz, shifted, padded, acc, w_all, w_t, oper,
    send_sem, recv_sem, halo_sem, w_send, w_recv, o_send, o_recv, pass_send,
):
    me = lax.axis_index("ctx")
    my_ch = lax.axis_index("ch")
    other_core = 2 * (my_ch // 2) + 1 - lax.rem(my_ch, 2)

    barrier = pltpu.get_barrier_semaphore()

    @pl.loop(1, ctx_n)
    def _(step):
        pl.semaphore_signal(
            barrier, inc=1, device_id={"ctx": lax.rem(me + step, ctx_n)}, device_id_type=MESH)

    @pl.loop(1, ch_n)
    def _(step):
        pl.semaphore_signal(
            barrier, inc=1, device_id={"ch": lax.rem(my_ch + step, ch_n)}, device_id_type=MESH)

    def pack(chunk, halves, dst):
        for half in range(2):
            for chan in range(2):
                flat[pl.ds(2 * chan + half, 64, stride=4), :] = halves[half][
                    64 * chan:64 * chan + 64, :]
        dst[chunk] = flat[...].reshape(ctx_n, 4, LANES).astype(BF16)

    def unpack(chunk, src):
        flat[...] = src[chunk].astype(F32).reshape(4 * ctx_n, LANES)

    def exchange(src, dst, which, chunk):
        @pl.loop(1, ctx_n)
        def _(step):
            target = lax.rem(me + step, ctx_n)
            remote(src.at[chunk, target], dst.at[chunk, me], send_sem.at[which, chunk],
                   recv_sem.at[which, chunk], "ctx", target).start()
        dst[chunk, me] = src[chunk, me]

    def arrived(dst, which, chunk):
        wait_bytes(dst.at[chunk, pl.ds(0, ctx_n - 1)], recv_sem.at[which, chunk])

    cuts = [slice(0, LANES), slice(LANES, 2 * LANES)]

    for chunk in range(2):
        pack(chunk, [filt_ref[cut, cuts[chunk]].T for cut in cuts], send_h)

    tails = [ref[240:256, :].astype(F32)[14:16] for ref in (q_ref, k_ref, v_ref)]
    halo_out[...] = jnp.concatenate(tails + [jnp.zeros((10, 256), F32)], axis=0).astype(BF16)
    for index, ref in enumerate((q_ref, k_ref, v_ref)):
        wide[index, pl.ds(8, 256), :] = ref[...].astype(F32)

    pl.semaphore_wait(barrier, ctx_n + ch_n - 2)

    ahead = lax.rem(me + 1, ctx_n)
    halo_copy = remote(halo_out, halo_in, halo_sem.at[0], halo_sem.at[1], "ctx", ahead)
    halo_copy.start()
    for chunk in range(2):
        exchange(send_h, recv_h, 0, chunk)

    @pl.loop(1, ch_n)
    def _(step):
        target = lax.rem(my_ch + step, ch_n)
        remote(w_ref.at[:, pl.ds(pl.multiple_of(target * 256, 256), 256)], w_all.at[my_ch],
               w_send, w_recv, "ch", target).start()
    w_all[my_ch] = w_ref[:, pl.ds(pl.multiple_of(my_ch * 256, 256), 256)]

    halo_copy.wait()
    before = jnp.where(me > 0, halo_in[...].astype(F32), 0.0)
    for index in range(3):
        wide[index, 6:8, :] = before[2 * index:2 * index + 2, :]

    def short(index, half, chunk):
        at, cut = half * LANES, cuts[chunk]
        return (
            taps_ref[index, 0:1, cut] * wide[index, pl.ds(6 + at, LANES), cut]
            + taps_ref[index, 1:2, cut] * wide[index, pl.ds(7 + at, LANES), cut]
            + taps_ref[index, 2:3, cut] * wide[index, pl.ds(8 + at, LANES), cut]
            + sbias_ref[index:index + 1, cut]
        )

    for chunk in range(2):
        for half in range(2):
            gated_t[chunk, half] = (short(1, half, chunk) * short(2, half, chunk)).T
        pack(chunk, [gated_t[chunk, 0], gated_t[chunk, 1]], send_g)
        exchange(send_g, recv_g, 1, chunk)

    for chunk in range(2):
        for half in range(2):
            query_t[chunk, half] = short(0, half, chunk).T

    for chunk in range(2):
        arrived(recv_h, 0, chunk)
        toeplitz_rows(recv_h, toeplitz, chunk, ctx_n)

    padded[0:STEP, :] = jnp.zeros((STEP, LANES), F32)
    for chunk in range(2):
        arrived(recv_g, 1, chunk)
        unpack(chunk, recv_g)
        for chan in range(2):
            for half in range(2):
                padded[pl.ds(STEP + half, 64, stride=2), :] = flat[
                    pl.ds(2 * chan + half, 64, stride=4), :]
            for lag in range(STEP):
                shifted[:, pl.ds(lag * LANES, LANES)] = padded[
                    pl.ds(STEP - lag, LANES), :].astype(BF16)
            for part in range(8):
                rows = LANES - STEP * part
                product = jnp.dot(
                    shifted[0:rows, :],
                    toeplitz[2 * chunk + chan, pl.ds(2048 * part, 2048), :],
                    preferred_element_type=F32)
                if part == 0:
                    acc[...] = product
                else:
                    acc[pl.ds(STEP * part, rows), :] += product
            for half in range(2):
                flat[pl.ds(2 * chan + half, 64, stride=4), :] = acc[pl.ds(half, 64, stride=2), :]
        send_y[chunk] = flat[...].reshape(ctx_n, 4, LANES).astype(BF16)
        exchange(send_y, recv_y, 2, chunk)

    wait_bytes(w_all.at[pl.ds(0, ch_n - 1)], w_recv)

    @pl.loop(0, ch_n)
    def _(index):
        for chunk in range(2):
            w_t[index, chunk] = w_all[index, cuts[chunk], :].T

    def pass_on(source, chunk, copy_sem, target):
        return remote(oper.at[source, chunk], oper.at[source, chunk], copy_sem,
                      o_recv.at[source, chunk], "ch", target)

    for chunk in range(2):
        skip_t = jnp.broadcast_to(skip_ref[:, cuts[chunk]], (LANES, LANES)).T
        arrived(recv_y, 2, chunk)
        unpack(chunk, recv_y)
        for half in range(2):
            conv = jnp.concatenate(
                [flat[pl.ds(2 * chan + half, 64, stride=4), :] for chan in range(2)], axis=0)
            oper[my_ch, chunk, :, cuts[half]] = (
                query_t[chunk, half] * (conv + skip_t * gated_t[chunk, half])).astype(BF16)
        for hop in (2, 6, 4):
            pass_on(my_ch, chunk, o_send, lax.rem(my_ch + hop, ch_n)).start()
        pass_on(my_ch, chunk, o_send, other_core).start()

    bias_t = jnp.broadcast_to(obias_ref[...], (LANES, 256)).T
    total = jnp.concatenate([bias_t, bias_t], axis=1)

    def add(total, source, chunk):
        return total + jnp.dot(w_t[source, chunk], oper[source, chunk], preferred_element_type=F32)

    for chunk in range(2):
        total = add(total, my_ch, chunk)
    for chunk in range(2):
        for hop in (2, 6, 4):
            source = lax.rem(my_ch + hop, ch_n)
            wait_bytes(oper.at[source, chunk], o_recv.at[source, chunk])
            pass_on(source, chunk, pass_send, other_core).start()
            total = add(total, source, chunk)
        for hop in (0, 2, 6, 4):
            source = lax.rem(other_core + hop, ch_n)
            wait_bytes(oper.at[source, chunk], o_recv.at[source, chunk])
            total = add(total, source, chunk)
    out_ref[...] = total.astype(BF16)

    for which, ref in enumerate((send_h, send_g, send_y)):
        for chunk in range(2):
            wait_bytes(ref.at[chunk, pl.ds(0, ctx_n - 1)], send_sem.at[which, chunk])
    wait_bytes(w_all.at[pl.ds(0, ch_n - 1)], w_send)
    wait_bytes(oper.at[pl.ds(0, 4)], o_send)
    wait_bytes(oper.at[pl.ds(0, 3)], pass_send)


def shards(q, k, v, taps, sbias, filt, skip, weight, obias):
    ctx_n, ch_n = lax.axis_size("ctx"), lax.axis_size("ch")
    vmem = pl.BlockSpec(memory_space=pltpu.VMEM)
    message = pltpu.VMEM((2, ctx_n, 4, LANES), BF16)
    dma = pltpu.SemaphoreType.DMA
    return pl.pallas_call(
        functools.partial(kernel, ctx_n, ch_n),
        out_shape=jax.ShapeDtypeStruct((256, 256), BF16),
        in_specs=[vmem] * 9,
        out_specs=vmem,
        scratch_shapes=[
            pltpu.VMEM((256, LANES), F32),
            pltpu.VMEM((16, 256), BF16),
            pltpu.VMEM((16, 256), BF16),
            pltpu.VMEM((3, 264, 256), F32),
            message, message, message, message, message, message,
            pltpu.VMEM((2, 2, LANES, LANES), F32),
            pltpu.VMEM((2, 2, LANES, LANES), F32),
            pltpu.VMEM((4, 16384, LANES), BF16),
            pltpu.VMEM((LANES, 2048), BF16),
            pltpu.VMEM((LANES + STEP, LANES), F32),
            pltpu.VMEM((LANES, LANES), F32),
            pltpu.VMEM((ch_n, 256, 256), BF16),
            pltpu.VMEM((ch_n, 2, 256, LANES), BF16),
            pltpu.VMEM((ch_n, 2, LANES, 256), BF16),
            dma((3, 2)), dma((3, 2)), dma((2,)), dma, dma, dma, dma((ch_n, 2)), dma,
        ],
        compiler_params=pltpu.CompilerParams(
            collective_id=3, has_side_effects=True, vmem_limit_bytes=50 * 2**20),
    )(q, k, v, taps, sbias, filt, skip.reshape(1, -1), weight, obias.reshape(1, -1))


def solution(mesh):
    return jax.shard_map(
        shards,
        mesh=mesh,
        in_specs=(
            P("ctx", "ch"),
            P("ctx", "ch"),
            P("ctx", "ch"),
            P(None, None, "ch"),
            P(None, "ch"),
            P("ctx", "ch"),
            P("ch"),
            P("ch", None),
            P("ch"),
        ),
        out_specs=P("ch", "ctx"),
        check_vma=False,
    )
```

```python
import functools

import jax
import jax.numpy as jnp
from jax import lax
from jax.experimental import pallas as pl
from jax.experimental.pallas import tpu as pltpu
from jax.sharding import PartitionSpec as P

MESH = pl.DeviceIdType.MESH
F32 = jnp.float32
BF16 = jnp.bfloat16
LANES = 128
STEP = 16
PHASE = 32


def remote(src, dst, send_sem, recv_sem, axis, target):
    return pltpu.make_async_remote_copy(
        src_ref=src, dst_ref=dst, send_sem=send_sem, recv_sem=recv_sem,
        device_id={axis: target}, device_id_type=MESH,
    )


def wait_bytes(ref, sem):
    pltpu.make_async_copy(ref, ref, sem).wait()


def toeplitz_rows(recv_h, toeplitz, chunk, blocks):
    rows = lax.broadcasted_iota(jnp.int32, (STEP, LANES), 0)
    lanes = lax.broadcasted_iota(jnp.int32, (STEP, LANES), 1)
    parts = PHASE // STEP
    keep = [(lanes >= rows) & (lanes < LANES - STEP * part) for part in range(parts)]
    per_step = 8

    def build(index, earlier):
        earlier = list(earlier)
        bases = {}
        for inner in range(per_step):
            lags = recv_h[chunk, per_step * index + inner].astype(F32)
            for row in range(4):
                bases[inner, row] = pltpu.roll(
                    jnp.broadcast_to(lags[row:row + 1, :], (STEP, LANES)), 0, 1,
                    stride=1, stride_axis=0).astype(BF16)
        for inner in range(per_step):
            for row in range(4):
                chan, half = row // 2, row % 2
                base = bases[inner, row]
                at = pl.multiple_of(PHASE * (2 * (per_step * index + inner) + half), PHASE)
                for part in range(parts):
                    mixed = jnp.where(keep[part], base, earlier[chan])
                    if part:
                        mixed = pltpu.roll(mixed, STEP * part, 1)
                    toeplitz[2 * chunk + chan, pl.ds(at + STEP * part, STEP), :] = mixed
                earlier[chan] = base
        return tuple(earlier)

    zero = jnp.zeros((STEP, LANES), BF16)
    lax.fori_loop(0, blocks // per_step, build, (zero, zero))


def channel_conv(blocks, phases, shifted, acc, toeplitz, chan):
    group = lax.broadcasted_iota(jnp.int32, (LANES, LANES), 1) // PHASE
    count = LANES // PHASE
    for turn in range(1, count):
        blocks[turn, pl.ds(STEP, LANES), :] = pltpu.roll(
            blocks[0, pl.ds(STEP, LANES), :], PHASE * turn, 1)
    for phase in range(count):
        value = blocks[(-phase) % count, pl.ds(STEP, LANES), :]
        for lag in range(1, count):
            value = jnp.where(
                group == lag, blocks[(lag - phase) % count, pl.ds(STEP - lag, LANES), :], value)
        phases[phase, pl.ds(STEP, LANES), :] = value
        for quad in range(STEP // count):
            shifted[phase, :, quad * LANES:(quad + 1) * LANES] = phases[
                phase, pl.ds(STEP - count * quad, LANES), :].astype(BF16)
    depth = STEP * PHASE
    for part in range(LANES // STEP):
        rows = LANES - STEP * part
        product = jnp.dot(
            shifted[:, 0:rows, :].reshape(count * rows, depth),
            toeplitz[chan, pl.ds(depth * part, depth), :],
            preferred_element_type=F32).reshape(count, rows, LANES)
        if part == 0:
            acc[:, pl.ds(8, LANES), :] = product
        else:
            acc[:, pl.ds(8 + STEP * part, rows), :] += product
    value = acc[0, pl.ds(8, LANES), :]
    for phase in range(1, count):
        value = value + pltpu.roll(
            jnp.where(group < count - phase, acc[phase, pl.ds(8, LANES), :],
                      acc[phase, pl.ds(7, LANES), :]), PHASE * phase, 1)
    return value


def kernel(
    ctx_n, ch_n,
    q_hbm, k_hbm, v_hbm, taps_hbm, sbias_hbm, filt_hbm, skip_hbm, w_ref, obias_hbm,
    out_ref,
    q_ref, k_ref, v_ref, taps_ref, sbias_ref, filt_ref, skip_ref, obias_ref,
    flat, halo_out, halo_in, wide, send_h, send_g, send_y, recv_h, recv_g, recv_y,
    gated_t, query_t, toeplitz, shifted, blocks, phases, result, acc, w_all, w_t, oper,
    send_sem, recv_sem, halo_sem, w_send, w_recv, o_send, o_recv, pass_send, in_sem,
):
    me = lax.axis_index("ctx")
    my_ch = lax.axis_index("ch")
    other_core = 2 * (my_ch // 2) + 1 - lax.rem(my_ch, 2)

    fetches = [
        pltpu.make_async_copy(src, dst, in_sem.at[index])
        for index, (src, dst) in enumerate((
            (filt_hbm, filt_ref), (q_hbm, q_ref), (k_hbm, k_ref), (v_hbm, v_ref),
            (taps_hbm, taps_ref), (sbias_hbm, sbias_ref), (skip_hbm, skip_ref),
            (obias_hbm, obias_ref),
            (w_ref.at[:, pl.ds(pl.multiple_of(my_ch * 256, 256), 256)], w_all.at[my_ch])))
    ]
    fetches[0].start()

    barrier = pltpu.get_barrier_semaphore()

    @pl.loop(1, ctx_n)
    def _(step):
        pl.semaphore_signal(
            barrier, inc=1, device_id={"ctx": lax.rem(me + step, ctx_n)}, device_id_type=MESH)

    @pl.loop(1, ch_n)
    def _(step):
        pl.semaphore_signal(
            barrier, inc=1, device_id={"ch": lax.rem(my_ch + step, ch_n)}, device_id_type=MESH)

    def pack(chunk, halves, dst):
        for half in range(2):
            for chan in range(2):
                flat[pl.ds(2 * chan + half, 64, stride=4), :] = halves[half][
                    64 * chan:64 * chan + 64, :]
        dst[chunk] = flat[...].reshape(ctx_n, 4, LANES).astype(BF16)

    def unpack(chunk, src):
        flat[...] = src[chunk].astype(F32).reshape(4 * ctx_n, LANES)

    def exchange(src, dst, which, chunk):
        @pl.loop(1, ctx_n)
        def _(step):
            target = lax.rem(me + step, ctx_n)
            remote(src.at[chunk, target], dst.at[chunk, me], send_sem.at[which, chunk],
                   recv_sem.at[which, chunk], "ctx", target).start()
        dst[chunk, me] = src[chunk, me]

    def arrived(dst, which, chunk):
        wait_bytes(dst.at[chunk, pl.ds(0, ctx_n - 1)], recv_sem.at[which, chunk])

    cuts = [slice(0, LANES), slice(LANES, 2 * LANES)]

    for fetch in fetches[1:]:
        fetch.start()
    for count in range(LANES // PHASE):
        blocks[count, 0:STEP, :] = jnp.zeros((STEP, LANES), F32)
        phases[count, 0:STEP, :] = jnp.zeros((STEP, LANES), F32)
        acc[count, 0:8, :] = jnp.zeros((8, LANES), F32)

    fetches[0].wait()
    for chunk in range(2):
        pack(chunk, [filt_ref[cut, cuts[chunk]].T for cut in cuts], send_h)

    for fetch in fetches[1:]:
        fetch.wait()
    tails = [ref[240:256, :].astype(F32)[14:16] for ref in (q_ref, k_ref, v_ref)]
    halo_out[...] = jnp.concatenate(tails + [jnp.zeros((10, 256), F32)], axis=0).astype(BF16)
    for index, ref in enumerate((q_ref, k_ref, v_ref)):
        wide[index, pl.ds(8, 256), :] = ref[...].astype(F32)

    pl.semaphore_wait(barrier, ctx_n + ch_n - 2)

    ahead = lax.rem(me + 1, ctx_n)
    halo_copy = remote(halo_out, halo_in, halo_sem.at[0], halo_sem.at[1], "ctx", ahead)
    halo_copy.start()
    for chunk in range(2):
        exchange(send_h, recv_h, 0, chunk)

    @pl.loop(1, ch_n)
    def _(step):
        target = lax.rem(my_ch + step, ch_n)
        remote(w_ref.at[:, pl.ds(pl.multiple_of(target * 256, 256), 256)], w_all.at[my_ch],
               w_send, w_recv, "ch", target).start()

    halo_copy.wait()
    before = jnp.where(me > 0, halo_in[...].astype(F32), 0.0)
    for index in range(3):
        wide[index, 6:8, :] = before[2 * index:2 * index + 2, :]

    def short(index, half, chunk):
        at, cut = half * LANES, cuts[chunk]
        return (
            taps_ref[index, 0:1, cut] * wide[index, pl.ds(6 + at, LANES), cut]
            + taps_ref[index, 1:2, cut] * wide[index, pl.ds(7 + at, LANES), cut]
            + taps_ref[index, 2:3, cut] * wide[index, pl.ds(8 + at, LANES), cut]
            + sbias_ref[index:index + 1, cut]
        )

    for chunk in range(2):
        for half in range(2):
            gated_t[chunk, half] = (short(1, half, chunk) * short(2, half, chunk)).T
        pack(chunk, [gated_t[chunk, 0], gated_t[chunk, 1]], send_g)
        exchange(send_g, recv_g, 1, chunk)

    for chunk in range(2):
        arrived(recv_h, 0, chunk)
        toeplitz_rows(recv_h, toeplitz, chunk, ctx_n)
        arrived(recv_g, 1, chunk)
        unpack(chunk, recv_g)
        for chan in range(2):
            for half in range(2):
                blocks[0, pl.ds(STEP + half, 64, stride=2), :] = flat[
                    pl.ds(2 * chan + half, 64, stride=4), :]
            result[...] = channel_conv(
                blocks, phases, shifted, acc, toeplitz, 2 * chunk + chan)
            for half in range(2):
                flat[pl.ds(2 * chan + half, 64, stride=4), :] = result[pl.ds(half, 64, stride=2), :]
        send_y[chunk] = flat[...].reshape(ctx_n, 4, LANES).astype(BF16)
        exchange(send_y, recv_y, 2, chunk)

    for chunk in range(2):
        for half in range(2):
            query_t[chunk, half] = short(0, half, chunk).T

    wait_bytes(w_all.at[pl.ds(0, ch_n - 1)], w_recv)

    @pl.loop(0, ch_n)
    def _(index):
        for chunk in range(2):
            w_t[index, chunk] = w_all[index, cuts[chunk], :].T

    def pass_on(source, chunk, copy_sem, target):
        return remote(oper.at[source, chunk], oper.at[source, chunk], copy_sem,
                      o_recv.at[source, chunk], "ch", target)

    for chunk in range(2):
        skip_t = jnp.broadcast_to(skip_ref[:, cuts[chunk]], (LANES, LANES)).T
        arrived(recv_y, 2, chunk)
        unpack(chunk, recv_y)
        for half in range(2):
            conv = jnp.concatenate(
                [flat[pl.ds(2 * chan + half, 64, stride=4), :] for chan in range(2)], axis=0)
            oper[my_ch, chunk, :, cuts[half]] = (
                query_t[chunk, half] * (conv + skip_t * gated_t[chunk, half])).astype(BF16)
        for hop in (2, 6, 4):
            pass_on(my_ch, chunk, o_send, lax.rem(my_ch + hop, ch_n)).start()
        pass_on(my_ch, chunk, o_send, other_core).start()

    bias_t = jnp.broadcast_to(obias_ref[...], (LANES, 256)).T
    total = jnp.concatenate([bias_t, bias_t], axis=1)

    def add(total, source, chunk):
        return total + jnp.dot(w_t[source, chunk], oper[source, chunk], preferred_element_type=F32)

    for chunk in range(2):
        total = add(total, my_ch, chunk)
    for chunk in range(2):
        for hop in (2, 6, 4):
            source = lax.rem(my_ch + hop, ch_n)
            wait_bytes(oper.at[source, chunk], o_recv.at[source, chunk])
            pass_on(source, chunk, pass_send, other_core).start()
            total = add(total, source, chunk)
        for hop in (0, 2, 6, 4):
            source = lax.rem(other_core + hop, ch_n)
            wait_bytes(oper.at[source, chunk], o_recv.at[source, chunk])
            total = add(total, source, chunk)
    out_ref[...] = total.astype(BF16)

    for which, ref in enumerate((send_h, send_g, send_y)):
        for chunk in range(2):
            wait_bytes(ref.at[chunk, pl.ds(0, ctx_n - 1)], send_sem.at[which, chunk])
    wait_bytes(w_all.at[pl.ds(0, ch_n - 1)], w_send)
    wait_bytes(oper.at[pl.ds(0, 4)], o_send)
    wait_bytes(oper.at[pl.ds(0, 3)], pass_send)


def shards(q, k, v, taps, sbias, filt, skip, weight, obias):
    ctx_n, ch_n = lax.axis_size("ctx"), lax.axis_size("ch")
    vmem = pl.BlockSpec(memory_space=pltpu.VMEM)
    message = pltpu.VMEM((2, ctx_n, 4, LANES), BF16)
    dma = pltpu.SemaphoreType.DMA
    return pl.pallas_call(
        functools.partial(kernel, ctx_n, ch_n),
        out_shape=jax.ShapeDtypeStruct((256, 256), BF16),
        in_specs=[pl.BlockSpec(memory_space=pl.ANY)] * 9,
        out_specs=vmem,
        scratch_shapes=[
            pltpu.VMEM((256, 256), BF16),
            pltpu.VMEM((256, 256), BF16),
            pltpu.VMEM((256, 256), BF16),
            pltpu.VMEM((3, 3, 256), F32),
            pltpu.VMEM((3, 256), F32),
            pltpu.VMEM((256, 256), F32),
            pltpu.VMEM((1, 256), F32),
            pltpu.VMEM((1, 256), F32),
            pltpu.VMEM((256, LANES), F32),
            pltpu.VMEM((16, 256), BF16),
            pltpu.VMEM((16, 256), BF16),
            pltpu.VMEM((3, 264, 256), F32),
            message, message, message, message, message, message,
            pltpu.VMEM((2, 2, LANES, LANES), F32),
            pltpu.VMEM((2, 2, LANES, LANES), F32),
            pltpu.VMEM((4, LANES * PHASE, LANES), BF16),
            pltpu.VMEM((LANES // PHASE, LANES, STEP * PHASE), BF16),
            pltpu.VMEM((LANES // PHASE, STEP + LANES, LANES), F32),
            pltpu.VMEM((LANES // PHASE, STEP + LANES, LANES), F32),
            pltpu.VMEM((LANES, LANES), F32),
            pltpu.VMEM((LANES // PHASE, 8 + LANES, LANES), F32),
            pltpu.VMEM((ch_n, 256, 256), BF16),
            pltpu.VMEM((ch_n, 2, 256, LANES), BF16),
            pltpu.VMEM((ch_n, 2, LANES, 256), BF16),
            dma((3, 2)), dma((3, 2)), dma((2,)), dma, dma, dma, dma((ch_n, 2)), dma, dma((9,)),
        ],
        compiler_params=pltpu.CompilerParams(
            collective_id=3, has_side_effects=True, vmem_limit_bytes=63 * 2**20),
    )(q, k, v, taps, sbias, filt, skip.reshape(1, -1), weight, obias.reshape(1, -1))


def solution(mesh):
    return jax.shard_map(
        shards,
        mesh=mesh,
        in_specs=(
            P("ctx", "ch"),
            P("ctx", "ch"),
            P("ctx", "ch"),
            P(None, None, "ch"),
            P(None, "ch"),
            P("ctx", "ch"),
            P("ch"),
            P("ch", None),
            P("ch"),
        ),
        out_specs=P("ch", "ctx"),
        check_vma=False,
    )
```

```python
import functools

import jax
import jax.numpy as jnp
from jax import lax
from jax.experimental import pallas as pl
from jax.experimental.pallas import tpu as pltpu
from jax.sharding import PartitionSpec as P

MESH = pl.DeviceIdType.MESH
F32 = jnp.float32
BF16 = jnp.bfloat16
LANES = 128
STEP = 16
PHASE = 32


def remote(src, dst, send_sem, recv_sem, axis, target):
    return pltpu.make_async_remote_copy(
        src_ref=src, dst_ref=dst, send_sem=send_sem, recv_sem=recv_sem,
        device_id={axis: target}, device_id_type=MESH,
    )


def wait_bytes(ref, sem):
    pltpu.make_async_copy(ref, ref, sem).wait()


def toeplitz_rows(recv_h, toeplitz, blocks):
    rows = lax.broadcasted_iota(jnp.int32, (STEP, LANES), 0)
    lanes = lax.broadcasted_iota(jnp.int32, (STEP, LANES), 1)
    parts = PHASE // STEP
    keep = [(lanes >= rows) & (lanes < LANES - STEP * part) for part in range(parts)]
    per_step = 4

    def build(index, earlier):
        earlier = list(earlier)
        bases = {}
        for inner in range(per_step):
            lags = recv_h[per_step * index + inner].astype(F32)
            for row in range(8):
                bases[inner, row] = pltpu.roll(
                    jnp.broadcast_to(lags[row:row + 1, :], (STEP, LANES)), 0, 1,
                    stride=1, stride_axis=0).astype(BF16)
        for inner in range(per_step):
            for row in range(8):
                chan, half = row // 2, row % 2
                base = bases[inner, row]
                at = pl.multiple_of(PHASE * (2 * (per_step * index + inner) + half), PHASE)
                for part in range(parts):
                    mixed = jnp.where(keep[part], base, earlier[chan])
                    if part:
                        mixed = pltpu.roll(mixed, STEP * part, 1)
                    toeplitz[chan, pl.ds(at + STEP * part, STEP), :] = mixed
                earlier[chan] = base
        return tuple(earlier)

    zero = jnp.zeros((STEP, LANES), BF16)
    lax.fori_loop(0, blocks // per_step, build, (zero,) * 4)


def channel_conv(blocks, phases, shifted, acc, toeplitz, chan):
    group = lax.broadcasted_iota(jnp.int32, (LANES, LANES), 1) // PHASE
    count = LANES // PHASE
    for turn in range(1, count):
        blocks[turn, pl.ds(STEP, LANES), :] = pltpu.roll(
            blocks[0, pl.ds(STEP, LANES), :], PHASE * turn, 1)
    for phase in range(count):
        value = blocks[(-phase) % count, pl.ds(STEP, LANES), :]
        for lag in range(1, count):
            value = jnp.where(
                group == lag, blocks[(lag - phase) % count, pl.ds(STEP - lag, LANES), :], value)
        phases[phase, pl.ds(STEP, LANES), :] = value
        for quad in range(STEP // count):
            shifted[phase, :, quad * LANES:(quad + 1) * LANES] = phases[
                phase, pl.ds(STEP - count * quad, LANES), :].astype(BF16)
    depth = STEP * PHASE
    for part in range(LANES // STEP):
        rows = LANES - STEP * part
        product = jnp.dot(
            shifted[:, 0:rows, :].reshape(count * rows, depth),
            toeplitz[chan, pl.ds(depth * part, depth), :],
            preferred_element_type=F32).reshape(count, rows, LANES)
        if part == 0:
            acc[:, pl.ds(8, LANES), :] = product
        else:
            acc[:, pl.ds(8 + STEP * part, rows), :] += product
    value = acc[0, pl.ds(8, LANES), :]
    for phase in range(1, count):
        value = value + pltpu.roll(
            jnp.where(group < count - phase, acc[phase, pl.ds(8, LANES), :],
                      acc[phase, pl.ds(7, LANES), :]), PHASE * phase, 1)
    return value


def kernel(
    ctx_n, ch_n,
    q_hbm, k_hbm, v_hbm, taps_hbm, sbias_hbm, filt_hbm, skip_hbm, w_ref, obias_hbm,
    out_ref,
    q_ref, k_ref, v_ref, taps_ref, sbias_ref, filt_ref, skip_ref, obias_ref,
    flat, wide_flat, halo_out, halo_in, wide, send_h, send_g, send_y, recv_h, recv_g, recv_y,
    gated_t, query_t, toeplitz, shifted, blocks, phases, result, acc, w_all, w_t, oper,
    send_sem, recv_sem, halo_sem, w_send, w_recv, o_send, o_recv, in_sem, h_sem,
):
    me = lax.axis_index("ctx")
    my_ch = lax.axis_index("ch")
    other_core = 2 * (my_ch // 2) + 1 - lax.rem(my_ch, 2)

    fetches = [
        pltpu.make_async_copy(src, dst, in_sem.at[index])
        for index, (src, dst) in enumerate((
            (filt_hbm, filt_ref), (q_hbm, q_ref), (k_hbm, k_ref), (v_hbm, v_ref),
            (taps_hbm, taps_ref), (sbias_hbm, sbias_ref), (skip_hbm, skip_ref),
            (obias_hbm, obias_ref),
            (w_ref.at[:, pl.ds(pl.multiple_of(my_ch * 256, 256), 256)], w_all.at[my_ch])))
    ]
    fetches[0].start()

    barrier = pltpu.get_barrier_semaphore()

    @pl.loop(1, ctx_n)
    def _(step):
        pl.semaphore_signal(
            barrier, inc=1, device_id={"ctx": lax.rem(me + step, ctx_n)}, device_id_type=MESH)

    @pl.loop(1, ch_n)
    def _(step):
        pl.semaphore_signal(
            barrier, inc=1, device_id={"ch": lax.rem(my_ch + step, ch_n)}, device_id_type=MESH)

    def pack(chunk, halves, dst):
        for half in range(2):
            for chan in range(2):
                flat[pl.ds(2 * chan + half, 64, stride=4), :] = halves[half][
                    64 * chan:64 * chan + 64, :]
        dst[chunk] = flat[...].reshape(ctx_n, 4, LANES).astype(BF16)

    def unpack(chunk, src):
        flat[...] = src[chunk].astype(F32).reshape(4 * ctx_n, LANES)

    def exchange(src, dst, which, chunk):
        @pl.loop(1, ctx_n)
        def _(step):
            target = lax.rem(me + step, ctx_n)
            remote(src.at[chunk, target], dst.at[chunk, me], send_sem.at[which, chunk],
                   recv_sem.at[which, chunk], "ctx", target).start()
        dst[chunk, me] = src[chunk, me]

    def arrived(dst, which, chunk):
        wait_bytes(dst.at[chunk, pl.ds(0, ctx_n - 1)], recv_sem.at[which, chunk])

    cuts = [slice(0, LANES), slice(LANES, 2 * LANES)]

    for fetch in fetches[1:]:
        fetch.start()
    for count in range(LANES // PHASE):
        blocks[count, 0:STEP, :] = jnp.zeros((STEP, LANES), F32)
        phases[count, 0:STEP, :] = jnp.zeros((STEP, LANES), F32)
        acc[count, 0:8, :] = jnp.zeros((8, LANES), F32)

    fetches[0].wait()
    for half in range(2):
        columns = filt_ref[cuts[half], :].T
        for chan in range(4):
            wide_flat[pl.ds(2 * chan + half, 64, stride=8), :] = columns[
                64 * chan:64 * chan + 64, :]
    send_h[...] = wide_flat[...].reshape(ctx_n, 8, LANES).astype(BF16)

    for fetch in fetches[1:]:
        fetch.wait()
    tails = [ref[240:256, :].astype(F32)[14:16] for ref in (k_ref, v_ref, q_ref)]
    halo_out[...] = jnp.concatenate(tails + [jnp.zeros((10, 256), F32)], axis=0).astype(BF16)

    pl.semaphore_wait(barrier, ctx_n + ch_n - 2)

    ahead = lax.rem(me + 1, ctx_n)
    halo_copy = remote(halo_out, halo_in, halo_sem.at[0], halo_sem.at[1], "ctx", ahead)
    halo_copy.start()

    @pl.loop(1, ctx_n)
    def _(step):
        target = lax.rem(me + step, ctx_n)
        remote(send_h.at[target], recv_h.at[me], h_sem.at[0], h_sem.at[1], "ctx", target).start()
    recv_h[me] = send_h[me]

    @pl.loop(1, ch_n)
    def _(step):
        target = lax.rem(my_ch + step, ch_n)
        remote(w_ref.at[:, pl.ds(pl.multiple_of(target * 256, 256), 256)], w_all.at[my_ch],
               w_send, w_recv, "ch", target).start()

    for index, ref in enumerate((k_ref, v_ref, q_ref)):
        wide[index, pl.ds(8, 256), :] = ref[...].astype(F32)
    halo_copy.wait()
    before = jnp.where(me > 0, halo_in[...].astype(F32), 0.0)
    for index in range(3):
        wide[index, 6:8, :] = before[2 * index:2 * index + 2, :]

    def short(index, half, chunk):
        at, cut, slot = half * LANES, cuts[chunk], (index + 2) % 3
        return (
            taps_ref[index, 0:1, cut] * wide[slot, pl.ds(6 + at, LANES), cut]
            + taps_ref[index, 1:2, cut] * wide[slot, pl.ds(7 + at, LANES), cut]
            + taps_ref[index, 2:3, cut] * wide[slot, pl.ds(8 + at, LANES), cut]
            + sbias_ref[index:index + 1, cut]
        )

    for chunk in range(2):
        for half in range(2):
            gated_t[chunk, half] = (short(1, half, chunk) * short(2, half, chunk)).T
        pack(chunk, [gated_t[chunk, 0], gated_t[chunk, 1]], send_g)
        exchange(send_g, recv_g, 0, chunk)

    wait_bytes(recv_h.at[pl.ds(0, ctx_n - 1)], h_sem.at[1])
    toeplitz_rows(recv_h, toeplitz, ctx_n)
    for chunk in range(2):
        arrived(recv_g, 0, chunk)
        unpack(chunk, recv_g)
        for chan in range(2):
            for half in range(2):
                blocks[0, pl.ds(STEP + half, 64, stride=2), :] = flat[
                    pl.ds(2 * chan + half, 64, stride=4), :]
            result[...] = channel_conv(
                blocks, phases, shifted, acc, toeplitz, 2 * chunk + chan)
            for half in range(2):
                flat[pl.ds(2 * chan + half, 64, stride=4), :] = result[pl.ds(half, 64, stride=2), :]
        send_y[chunk] = flat[...].reshape(ctx_n, 4, LANES).astype(BF16)
        exchange(send_y, recv_y, 1, chunk)

    for chunk in range(2):
        for half in range(2):
            query_t[chunk, half] = short(0, half, chunk).T

    wait_bytes(w_all.at[pl.ds(0, ch_n - 1)], w_recv)

    @pl.loop(0, ch_n)
    def _(index):
        for chunk in range(2):
            w_t[index, chunk] = w_all[index, cuts[chunk], :].T

    def pass_on(source, chunk, copy_sem, target):
        return remote(oper.at[source, chunk], oper.at[source, chunk], copy_sem,
                      o_recv.at[source, chunk], "ch", target)

    for chunk in range(2):
        skip_t = jnp.broadcast_to(skip_ref[:, cuts[chunk]], (LANES, LANES)).T
        arrived(recv_y, 1, chunk)
        unpack(chunk, recv_y)
        for half in range(2):
            conv = jnp.concatenate(
                [flat[pl.ds(2 * chan + half, 64, stride=4), :] for chan in range(2)], axis=0)
            oper[my_ch, chunk, :, cuts[half]] = (
                query_t[chunk, half] * (conv + skip_t * gated_t[chunk, half])).astype(BF16)
        for hop in (4, 3, 5, 2, 6, 1, 7):
            pass_on(my_ch, chunk, o_send, lax.rem(my_ch + hop, ch_n)).start()

    bias_t = jnp.broadcast_to(obias_ref[...], (LANES, 256)).T
    total = jnp.concatenate([bias_t, bias_t], axis=1)

    def add(total, source, chunk):
        return total + jnp.dot(w_t[source, chunk], oper[source, chunk], preferred_element_type=F32)

    for chunk in range(2):
        total = add(total, my_ch, chunk)
    for chunk in range(2):
        for hop in (1, 7, 2, 6, 3, 5, 4):
            source = lax.rem(my_ch + hop, ch_n)
            wait_bytes(oper.at[source, chunk], o_recv.at[source, chunk])
            total = add(total, source, chunk)
    out_ref[...] = total.astype(BF16)

    wait_bytes(send_h.at[pl.ds(0, ctx_n - 1)], h_sem.at[0])
    for which, ref in enumerate((send_g, send_y)):
        for chunk in range(2):
            wait_bytes(ref.at[chunk, pl.ds(0, ctx_n - 1)], send_sem.at[which, chunk])
    wait_bytes(w_all.at[pl.ds(0, ch_n - 1)], w_send)
    wait_bytes(oper.at[pl.ds(0, 7)], o_send)


def shards(q, k, v, taps, sbias, filt, skip, weight, obias):
    ctx_n, ch_n = lax.axis_size("ctx"), lax.axis_size("ch")
    vmem = pl.BlockSpec(memory_space=pltpu.VMEM)
    message = pltpu.VMEM((2, ctx_n, 4, LANES), BF16)
    dma = pltpu.SemaphoreType.DMA
    return pl.pallas_call(
        functools.partial(kernel, ctx_n, ch_n),
        out_shape=jax.ShapeDtypeStruct((256, 256), BF16),
        in_specs=[pl.BlockSpec(memory_space=pl.ANY)] * 9,
        out_specs=vmem,
        scratch_shapes=[
            pltpu.VMEM((256, 256), BF16),
            pltpu.VMEM((256, 256), BF16),
            pltpu.VMEM((256, 256), BF16),
            pltpu.VMEM((3, 3, 256), F32),
            pltpu.VMEM((3, 256), F32),
            pltpu.VMEM((256, 256), F32),
            pltpu.VMEM((1, 256), F32),
            pltpu.VMEM((1, 256), F32),
            pltpu.VMEM((256, LANES), F32),
            pltpu.VMEM((512, LANES), F32),
            pltpu.VMEM((16, 256), BF16),
            pltpu.VMEM((16, 256), BF16),
            pltpu.VMEM((3, 264, 256), F32),
            pltpu.VMEM((ctx_n, 8, LANES), BF16), message, message,
            pltpu.VMEM((ctx_n, 8, LANES), BF16), message, message,
            pltpu.VMEM((2, 2, LANES, LANES), F32),
            pltpu.VMEM((2, 2, LANES, LANES), F32),
            pltpu.VMEM((4, LANES * PHASE, LANES), BF16),
            pltpu.VMEM((LANES // PHASE, LANES, STEP * PHASE), BF16),
            pltpu.VMEM((LANES // PHASE, STEP + LANES, LANES), F32),
            pltpu.VMEM((LANES // PHASE, STEP + LANES, LANES), F32),
            pltpu.VMEM((LANES, LANES), F32),
            pltpu.VMEM((LANES // PHASE, 8 + LANES, LANES), F32),
            pltpu.VMEM((ch_n, 256, 256), BF16),
            pltpu.VMEM((ch_n, 2, 256, LANES), BF16),
            pltpu.VMEM((ch_n, 2, LANES, 256), BF16),
            dma((2, 2)), dma((2, 2)), dma((2,)), dma, dma, dma, dma((ch_n, 2)), dma((9,)), dma((2,)),
        ],
        compiler_params=pltpu.CompilerParams(
            collective_id=3, has_side_effects=True, vmem_limit_bytes=63 * 2**20),
    )(q, k, v, taps, sbias, filt, skip.reshape(1, -1), weight, obias.reshape(1, -1))


def solution(mesh):
    return jax.shard_map(
        shards,
        mesh=mesh,
        in_specs=(
            P("ctx", "ch"),
            P("ctx", "ch"),
            P("ctx", "ch"),
            P(None, None, "ch"),
            P(None, "ch"),
            P("ctx", "ch"),
            P("ch"),
            P("ch", None),
            P("ch"),
        ),
        out_specs=P("ch", "ctx"),
        check_vma=False,
    )
```

```python
import functools

import jax
import jax.numpy as jnp
from jax import lax
from jax.experimental import pallas as pl
from jax.experimental.pallas import tpu as pltpu
from jax.sharding import PartitionSpec as P

MESH = pl.DeviceIdType.MESH
F32 = jnp.float32
BF16 = jnp.bfloat16
LANES = 128
STEP = 16
PHASE = 32


def remote(src, dst, send_sem, recv_sem, axis, target):
    return pltpu.make_async_remote_copy(
        src_ref=src, dst_ref=dst, send_sem=send_sem, recv_sem=recv_sem,
        device_id={axis: target}, device_id_type=MESH,
    )


def wait_bytes(ref, sem):
    pltpu.make_async_copy(ref, ref, sem).wait()


def toeplitz_rows(recv_h, toeplitz, blocks):
    rows = lax.broadcasted_iota(jnp.int32, (STEP, LANES), 0)
    lanes = lax.broadcasted_iota(jnp.int32, (STEP, LANES), 1)
    parts = PHASE // STEP
    keep = [(lanes >= rows) & (lanes < LANES - STEP * part) for part in range(parts)]
    per_step = 4

    def build(index, earlier):
        earlier = list(earlier)
        bases = {}
        for inner in range(per_step):
            lags = recv_h[per_step * index + inner].astype(F32)
            for row in range(8):
                bases[inner, row] = pltpu.roll(
                    jnp.broadcast_to(lags[row:row + 1, :], (STEP, LANES)), 0, 1,
                    stride=1, stride_axis=0).astype(BF16)
        for inner in range(per_step):
            for row in range(8):
                chan, half = row // 2, row % 2
                base = bases[inner, row]
                at = pl.multiple_of(PHASE * (2 * (per_step * index + inner) + half), PHASE)
                for part in range(parts):
                    mixed = jnp.where(keep[part], base, earlier[chan])
                    if part:
                        mixed = pltpu.roll(mixed, STEP * part, 1)
                    toeplitz[chan, pl.ds(at + STEP * part, STEP), :] = mixed
                earlier[chan] = base
        return tuple(earlier)

    zero = jnp.zeros((STEP, LANES), BF16)
    lax.fori_loop(0, blocks // per_step, build, (zero,) * 4)


def channel_conv(blocks, phases, shifted, acc, toeplitz, chan):
    group = lax.broadcasted_iota(jnp.int32, (LANES, LANES), 1) // PHASE
    count = LANES // PHASE
    for turn in range(1, count):
        blocks[turn, pl.ds(STEP, LANES), :] = pltpu.roll(
            blocks[0, pl.ds(STEP, LANES), :], PHASE * turn, 1)
    for phase in range(count):
        value = blocks[(-phase) % count, pl.ds(STEP, LANES), :]
        for lag in range(1, count):
            value = jnp.where(
                group == lag, blocks[(lag - phase) % count, pl.ds(STEP - lag, LANES), :], value)
        phases[phase, pl.ds(STEP, LANES), :] = value
        for quad in range(STEP // count):
            shifted[phase, :, quad * LANES:(quad + 1) * LANES] = phases[
                phase, pl.ds(STEP - count * quad, LANES), :].astype(BF16)
    depth = STEP * PHASE
    for part in range(LANES // STEP):
        rows = LANES - STEP * part
        product = jnp.dot(
            shifted[:, 0:rows, :].reshape(count * rows, depth),
            toeplitz[chan, pl.ds(depth * part, depth), :],
            preferred_element_type=F32).reshape(count, rows, LANES)
        if part == 0:
            acc[:, pl.ds(8, LANES), :] = product
        else:
            acc[:, pl.ds(8 + STEP * part, rows), :] += product
    value = acc[0, pl.ds(8, LANES), :]
    for phase in range(1, count):
        value = value + pltpu.roll(
            jnp.where(group < count - phase, acc[phase, pl.ds(8, LANES), :],
                      acc[phase, pl.ds(7, LANES), :]), PHASE * phase, 1)
    return value


def kernel(
    ctx_n, ch_n,
    q_hbm, k_hbm, v_hbm, filt_hbm, w_ref, small_hbm,
    out_ref,
    q_ref, k_ref, v_ref, filt_ref, small_ref,
    flat, wide_flat, halo_out, halo_in, wide, send_h, send_g, send_y, recv_h, recv_g, recv_y,
    gated_t, query_t, toeplitz, shifted, blocks, phases, result, acc, w_all, w_t, oper,
    send_sem, recv_sem, halo_sem, w_send, w_recv, o_send, o_recv, in_sem, h_sem,
):
    me = lax.axis_index("ctx")
    my_ch = lax.axis_index("ch")
    other_core = 2 * (my_ch // 2) + 1 - lax.rem(my_ch, 2)

    fetches = [
        pltpu.make_async_copy(src, dst, in_sem.at[index])
        for index, (src, dst) in enumerate((
            (filt_hbm, filt_ref), (q_hbm, q_ref), (k_hbm, k_ref), (v_hbm, v_ref),
            (small_hbm, small_ref),
            (w_ref.at[:, pl.ds(pl.multiple_of(my_ch * 256, 256), 256)], w_all.at[my_ch])))
    ]
    fetches[0].start()

    barrier = pltpu.get_barrier_semaphore()

    @pl.loop(1, ctx_n)
    def _(step):
        pl.semaphore_signal(
            barrier, inc=1, device_id={"ctx": lax.rem(me + step, ctx_n)}, device_id_type=MESH)

    @pl.loop(1, ch_n)
    def _(step):
        pl.semaphore_signal(
            barrier, inc=1, device_id={"ch": lax.rem(my_ch + step, ch_n)}, device_id_type=MESH)

    def pack(chunk, halves, dst):
        for half in range(2):
            for chan in range(2):
                flat[pl.ds(2 * chan + half, 64, stride=4), :] = halves[half][
                    64 * chan:64 * chan + 64, :]
        dst[chunk] = flat[...].reshape(ctx_n, 4, LANES).astype(BF16)

    def unpack(chunk, src):
        flat[...] = src[chunk].astype(F32).reshape(4 * ctx_n, LANES)

    def exchange(src, dst, which, chunk):
        @pl.loop(1, ctx_n)
        def _(step):
            target = lax.rem(me + 25 * step, ctx_n)
            remote(src.at[chunk, target], dst.at[chunk, me], send_sem.at[which, chunk],
                   recv_sem.at[which, chunk], "ctx", target).start()
        dst[chunk, me] = src[chunk, me]

    def arrived(dst, which, chunk):
        wait_bytes(dst.at[chunk, pl.ds(0, ctx_n - 1)], recv_sem.at[which, chunk])

    cuts = [slice(0, LANES), slice(LANES, 2 * LANES)]

    for fetch in fetches[1:]:
        fetch.start()
    for count in range(LANES // PHASE):
        blocks[count, 0:STEP, :] = jnp.zeros((STEP, LANES), F32)
        phases[count, 0:STEP, :] = jnp.zeros((STEP, LANES), F32)
        acc[count, 0:8, :] = jnp.zeros((8, LANES), F32)

    fetches[0].wait()
    for half in range(2):
        columns = filt_ref[cuts[half], :].T
        for chan in range(4):
            wide_flat[pl.ds(2 * chan + half, 64, stride=8), :] = columns[
                64 * chan:64 * chan + 64, :]
    send_h[...] = wide_flat[...].reshape(ctx_n, 8, LANES).astype(BF16)

    for fetch in fetches[1:]:
        fetch.wait()
    tails = [ref[240:256, :].astype(F32)[14:16] for ref in (k_ref, v_ref, q_ref)]
    halo_out[...] = jnp.concatenate(tails + [jnp.zeros((10, 256), F32)], axis=0).astype(BF16)

    pl.semaphore_wait(barrier, ctx_n + ch_n - 2)

    ahead = lax.rem(me + 1, ctx_n)
    halo_copy = remote(halo_out, halo_in, halo_sem.at[0], halo_sem.at[1], "ctx", ahead)
    halo_copy.start()

    @pl.loop(1, ctx_n)
    def _(step):
        target = lax.rem(me + 25 * step, ctx_n)
        remote(send_h.at[target], recv_h.at[me], h_sem.at[0], h_sem.at[1], "ctx", target).start()
    recv_h[me] = send_h[me]

    @pl.loop(1, ch_n)
    def _(step):
        target = lax.rem(my_ch + step, ch_n)
        remote(w_ref.at[:, pl.ds(pl.multiple_of(target * 256, 256), 256)], w_all.at[my_ch],
               w_send, w_recv, "ch", target).start()

    for index, ref in enumerate((k_ref, v_ref, q_ref)):
        wide[index, pl.ds(8, 256), :] = ref[...].astype(F32)
    halo_copy.wait()
    before = jnp.where(me > 0, halo_in[...].astype(F32), 0.0)
    for index in range(3):
        wide[index, 6:8, :] = before[2 * index:2 * index + 2, :]

    def short(index, half, chunk):
        at, cut, slot = half * LANES, cuts[chunk], (index + 2) % 3
        return (
            small_ref[pl.ds(3 * index + 0, 1), cut] * wide[slot, pl.ds(6 + at, LANES), cut]
            + small_ref[pl.ds(3 * index + 1, 1), cut] * wide[slot, pl.ds(7 + at, LANES), cut]
            + small_ref[pl.ds(3 * index + 2, 1), cut] * wide[slot, pl.ds(8 + at, LANES), cut]
            + small_ref[pl.ds(9 + index, 1), cut]
        )

    for chunk in range(2):
        for half in range(2):
            gated_t[chunk, half] = (short(1, half, chunk) * short(2, half, chunk)).T
        pack(chunk, [gated_t[chunk, 0], gated_t[chunk, 1]], send_g)
        exchange(send_g, recv_g, 0, chunk)

    wait_bytes(recv_h.at[pl.ds(0, ctx_n - 1)], h_sem.at[1])
    toeplitz_rows(recv_h, toeplitz, ctx_n)
    for chunk in range(2):
        arrived(recv_g, 0, chunk)
        unpack(chunk, recv_g)
        for chan in range(2):
            for half in range(2):
                blocks[0, pl.ds(STEP + half, 64, stride=2), :] = flat[
                    pl.ds(2 * chan + half, 64, stride=4), :]
            result[...] = channel_conv(
                blocks, phases, shifted, acc, toeplitz, 2 * chunk + chan)
            for half in range(2):
                flat[pl.ds(2 * chan + half, 64, stride=4), :] = result[pl.ds(half, 64, stride=2), :]
        send_y[chunk] = flat[...].reshape(ctx_n, 4, LANES).astype(BF16)
        exchange(send_y, recv_y, 1, chunk)

    for chunk in range(2):
        for half in range(2):
            query_t[chunk, half] = short(0, half, chunk).T

    wait_bytes(w_all.at[pl.ds(0, ch_n - 1)], w_recv)

    @pl.loop(0, ch_n)
    def _(index):
        for chunk in range(2):
            w_t[index, chunk] = w_all[index, cuts[chunk], :].T

    def pass_on(source, chunk, copy_sem, target):
        return remote(oper.at[source, chunk], oper.at[source, chunk], copy_sem,
                      o_recv.at[source, chunk], "ch", target)

    for chunk in range(2):
        skip_t = jnp.broadcast_to(small_ref[12:13, cuts[chunk]], (LANES, LANES)).T
        arrived(recv_y, 1, chunk)
        unpack(chunk, recv_y)
        for half in range(2):
            conv = jnp.concatenate(
                [flat[pl.ds(2 * chan + half, 64, stride=4), :] for chan in range(2)], axis=0)
            oper[my_ch, chunk, :, cuts[half]] = (
                query_t[chunk, half] * (conv + skip_t * gated_t[chunk, half])).astype(BF16)
        for hop in (4, 3, 5, 2, 6, 1, 7):
            pass_on(my_ch, chunk, o_send, lax.rem(my_ch + hop, ch_n)).start()

    bias_t = jnp.broadcast_to(small_ref[13:14, :], (LANES, 256)).T
    total = jnp.concatenate([bias_t, bias_t], axis=1)

    def add(total, source, chunk):
        return total + jnp.dot(w_t[source, chunk], oper[source, chunk], preferred_element_type=F32)

    for chunk in range(2):
        total = add(total, my_ch, chunk)
    for chunk in range(2):
        for hop in (1, 7, 2, 6, 3, 5, 4):
            source = lax.rem(my_ch + hop, ch_n)
            wait_bytes(oper.at[source, chunk], o_recv.at[source, chunk])
            total = add(total, source, chunk)
    out_ref[...] = total.astype(BF16)

    wait_bytes(send_h.at[pl.ds(0, ctx_n - 1)], h_sem.at[0])
    for which, ref in enumerate((send_g, send_y)):
        for chunk in range(2):
            wait_bytes(ref.at[chunk, pl.ds(0, ctx_n - 1)], send_sem.at[which, chunk])
    wait_bytes(w_all.at[pl.ds(0, ch_n - 1)], w_send)
    wait_bytes(oper.at[pl.ds(0, 7)], o_send)


def shards(q, k, v, taps, sbias, filt, skip, weight, obias):
    ctx_n, ch_n = lax.axis_size("ctx"), lax.axis_size("ch")
    vmem = pl.BlockSpec(memory_space=pltpu.VMEM)
    message = pltpu.VMEM((2, ctx_n, 4, LANES), BF16)
    dma = pltpu.SemaphoreType.DMA
    small = jnp.concatenate(
        [taps.reshape(9, -1), sbias, skip.reshape(1, -1), obias.reshape(1, -1)], axis=0)
    return pl.pallas_call(
        functools.partial(kernel, ctx_n, ch_n),
        out_shape=jax.ShapeDtypeStruct((256, 256), BF16),
        in_specs=[pl.BlockSpec(memory_space=pl.ANY)] * 6,
        out_specs=vmem,
        scratch_shapes=[
            pltpu.VMEM((256, 256), BF16),
            pltpu.VMEM((256, 256), BF16),
            pltpu.VMEM((256, 256), BF16),
            pltpu.VMEM((256, 256), F32),
            pltpu.VMEM((14, 256), F32),
            pltpu.VMEM((256, LANES), F32),
            pltpu.VMEM((512, LANES), F32),
            pltpu.VMEM((16, 256), BF16),
            pltpu.VMEM((16, 256), BF16),
            pltpu.VMEM((3, 264, 256), F32),
            pltpu.VMEM((ctx_n, 8, LANES), BF16), message, message,
            pltpu.VMEM((ctx_n, 8, LANES), BF16), message, message,
            pltpu.VMEM((2, 2, LANES, LANES), F32),
            pltpu.VMEM((2, 2, LANES, LANES), F32),
            pltpu.VMEM((4, LANES * PHASE, LANES), BF16),
            pltpu.VMEM((LANES // PHASE, LANES, STEP * PHASE), BF16),
            pltpu.VMEM((LANES // PHASE, STEP + LANES, LANES), F32),
            pltpu.VMEM((LANES // PHASE, STEP + LANES, LANES), F32),
            pltpu.VMEM((LANES, LANES), F32),
            pltpu.VMEM((LANES // PHASE, 8 + LANES, LANES), F32),
            pltpu.VMEM((ch_n, 256, 256), BF16),
            pltpu.VMEM((ch_n, 2, 256, LANES), BF16),
            pltpu.VMEM((ch_n, 2, LANES, 256), BF16),
            dma((2, 2)), dma((2, 2)), dma((2,)), dma, dma, dma, dma((ch_n, 2)), dma((6,)), dma((2,)),
        ],
        compiler_params=pltpu.CompilerParams(
            collective_id=3, has_side_effects=True, vmem_limit_bytes=54 * 2**20 - 256 * 1024),
    )(q, k, v, filt, weight, small)


def solution(mesh):
    return jax.shard_map(
        shards,
        mesh=mesh,
        in_specs=(
            P("ctx", "ch"),
            P("ctx", "ch"),
            P("ctx", "ch"),
            P(None, None, "ch"),
            P(None, "ch"),
            P("ctx", "ch"),
            P("ch"),
            P("ch", None),
            P("ch"),
        ),
        out_specs=P("ch", "ctx"),
        check_vma=False,
    )
```

```python
import functools

import jax
import jax.numpy as jnp
from jax import lax
from jax.experimental import pallas as pl
from jax.experimental.pallas import tpu as pltpu
from jax.sharding import PartitionSpec as P

MESH = pl.DeviceIdType.MESH
F32 = jnp.float32
BF16 = jnp.bfloat16
LANES = 128
STEP = 16
PHASE = 32


def remote(src, dst, send_sem, recv_sem, axis, target):
    return pltpu.make_async_remote_copy(
        src_ref=src, dst_ref=dst, send_sem=send_sem, recv_sem=recv_sem,
        device_id={axis: target}, device_id_type=MESH,
    )


def wait_bytes(ref, sem):
    pltpu.make_async_copy(ref, ref, sem).wait()


def toeplitz_rows(recv_h, toeplitz, blocks):
    rows = lax.broadcasted_iota(jnp.int32, (STEP, LANES), 0)
    lanes = lax.broadcasted_iota(jnp.int32, (STEP, LANES), 1)
    parts = PHASE // STEP
    keep = [(lanes >= rows) & (lanes < LANES - STEP * part) for part in range(parts)]
    per_step = 4

    def build(index, earlier):
        earlier = list(earlier)
        bases = {}
        for inner in range(per_step):
            lags = recv_h[per_step * index + inner].astype(F32)
            for row in range(8):
                bases[inner, row] = pltpu.roll(
                    jnp.broadcast_to(lags[row:row + 1, :], (STEP, LANES)), 0, 1,
                    stride=1, stride_axis=0).astype(BF16)
        for inner in range(per_step):
            for row in range(8):
                chan, half = row // 2, row % 2
                base = bases[inner, row]
                at = pl.multiple_of(PHASE * (2 * (per_step * index + inner) + half), PHASE)
                for part in range(parts):
                    mixed = jnp.where(keep[part], base, earlier[chan])
                    if part:
                        mixed = pltpu.roll(mixed, STEP * part, 1)
                    toeplitz[chan, pl.ds(at + STEP * part, STEP), :] = mixed
                earlier[chan] = base
        return tuple(earlier)

    zero = jnp.zeros((STEP, LANES), BF16)
    lax.fori_loop(0, blocks // per_step, build, (zero,) * 4)


def channel_conv(blocks, phases, shifted, acc, toeplitz, chan):
    group = lax.broadcasted_iota(jnp.int32, (LANES, LANES), 1) // PHASE
    count = LANES // PHASE
    for turn in range(1, count):
        blocks[turn, pl.ds(STEP, LANES), :] = pltpu.roll(
            blocks[0, pl.ds(STEP, LANES), :], PHASE * turn, 1)
    for phase in range(count):
        value = blocks[(-phase) % count, pl.ds(STEP, LANES), :]
        for lag in range(1, count):
            value = jnp.where(
                group == lag, blocks[(lag - phase) % count, pl.ds(STEP - lag, LANES), :], value)
        phases[phase, pl.ds(STEP, LANES), :] = value
        for quad in range(STEP // count):
            shifted[phase, :, quad * LANES:(quad + 1) * LANES] = phases[
                phase, pl.ds(STEP - count * quad, LANES), :].astype(BF16)
    depth = STEP * PHASE
    for part in range(LANES // STEP):
        rows = LANES - STEP * part
        product = jnp.dot(
            shifted[:, 0:rows, :].reshape(count * rows, depth),
            toeplitz[chan, pl.ds(depth * part, depth), :],
            preferred_element_type=F32).reshape(count, rows, LANES)
        if part == 0:
            acc[:, pl.ds(8, LANES), :] = product
        else:
            acc[:, pl.ds(8 + STEP * part, rows), :] += product
    value = acc[0, pl.ds(8, LANES), :]
    for phase in range(1, count):
        value = value + pltpu.roll(
            jnp.where(group < count - phase, acc[phase, pl.ds(8, LANES), :],
                      acc[phase, pl.ds(7, LANES), :]), PHASE * phase, 1)
    return value


def kernel(
    ctx_n, ch_n,
    q_hbm, k_hbm, v_hbm, filt_hbm, w_ref, small_hbm,
    out_ref,
    q_ref, k_ref, v_ref, filt_ref, small_ref,
    flat, wide_flat, halo_out, halo_in, wide, send_h, send_g, send_y, recv_h, recv_g, recv_y,
    gated_t, query_t, toeplitz, shifted, blocks, phases, result, acc, w_all, w_t, oper,
    send_sem, recv_sem, halo_sem, w_send, w_recv, o_send, o_recv, in_sem, h_sem,
):
    me = lax.axis_index("ctx")
    my_ch = lax.axis_index("ch")
    other_core = 2 * (my_ch // 2) + 1 - lax.rem(my_ch, 2)

    fetches = [
        pltpu.make_async_copy(src, dst, in_sem.at[index])
        for index, (src, dst) in enumerate((
            (filt_hbm, filt_ref), (q_hbm, q_ref), (k_hbm, k_ref), (v_hbm, v_ref),
            (small_hbm, small_ref),
            (w_ref.at[:, pl.ds(pl.multiple_of(my_ch * 256, 256), 256)], w_all.at[my_ch])))
    ]
    fetches[0].start()

    barrier = pltpu.get_barrier_semaphore()

    @pl.loop(1, ctx_n)
    def _(step):
        pl.semaphore_signal(
            barrier, inc=1, device_id={"ctx": lax.rem(me + step, ctx_n)}, device_id_type=MESH)

    @pl.loop(1, ch_n)
    def _(step):
        pl.semaphore_signal(
            barrier, inc=1, device_id={"ch": lax.rem(my_ch + step, ch_n)}, device_id_type=MESH)

    def pack(chunk, halves, dst):
        for half in range(2):
            for chan in range(2):
                flat[pl.ds(2 * chan + half, 64, stride=4), :] = halves[half][
                    64 * chan:64 * chan + 64, :]
        dst[chunk] = flat[...].reshape(ctx_n, 4, LANES).astype(BF16)

    def unpack(chunk, src):
        flat[...] = src[chunk].astype(F32).reshape(4 * ctx_n, LANES)

    def exchange(src, dst, which, chunk):
        @pl.loop(1, ctx_n)
        def _(step):
            target = lax.rem(me + 25 * step, ctx_n)
            remote(src.at[chunk, target], dst.at[chunk, me], send_sem.at[which, chunk],
                   recv_sem.at[which, chunk], "ctx", target).start()
        dst[chunk, me] = src[chunk, me]

    def arrived(dst, which, chunk):
        wait_bytes(dst.at[chunk, pl.ds(0, ctx_n - 1)], recv_sem.at[which, chunk])

    cuts = [slice(0, LANES), slice(LANES, 2 * LANES)]

    for fetch in fetches[1:]:
        fetch.start()
    for count in range(LANES // PHASE):
        blocks[count, 0:STEP, :] = jnp.zeros((STEP, LANES), F32)
        phases[count, 0:STEP, :] = jnp.zeros((STEP, LANES), F32)
        acc[count, 0:8, :] = jnp.zeros((8, LANES), F32)

    fetches[0].wait()
    for half in range(2):
        columns = filt_ref[cuts[half], :].T
        for chan in range(4):
            wide_flat[pl.ds(2 * chan + half, 64, stride=8), :] = columns[
                64 * chan:64 * chan + 64, :]
    send_h[...] = wide_flat[...].reshape(ctx_n, 8, LANES).astype(BF16)

    for fetch in fetches[1:]:
        fetch.wait()
    tails = [ref[240:256, :].astype(F32)[14:16] for ref in (k_ref, v_ref, q_ref)]
    halo_out[...] = jnp.concatenate(tails + [jnp.zeros((10, 256), F32)], axis=0).astype(BF16)

    pl.semaphore_wait(barrier, ctx_n + ch_n - 2)

    ahead = lax.rem(me + 1, ctx_n)
    halo_copy = remote(halo_out, halo_in, halo_sem.at[0], halo_sem.at[1], "ctx", ahead)
    halo_copy.start()

    @pl.loop(1, ctx_n)
    def _(step):
        target = lax.rem(me + 25 * step, ctx_n)
        remote(send_h.at[target], recv_h.at[me], h_sem.at[0], h_sem.at[1], "ctx", target).start()
    recv_h[me] = send_h[me]

    @pl.loop(1, ch_n)
    def _(step):
        target = lax.rem(my_ch + step, ch_n)
        remote(w_ref.at[:, pl.ds(pl.multiple_of(target * 256, 256), 256)], w_all.at[my_ch],
               w_send, w_recv, "ch", target).start()

    for index, ref in enumerate((k_ref, v_ref, q_ref)):
        wide[index, pl.ds(8, 256), :] = ref[...].astype(F32)
    halo_copy.wait()
    before = jnp.where(me > 0, halo_in[...].astype(F32), 0.0)
    for index in range(3):
        wide[index, 6:8, :] = before[2 * index:2 * index + 2, :]

    def short(index, half, chunk):
        at, cut, slot = half * LANES, cuts[chunk], (index + 2) % 3
        return (
            small_ref[index, 0:1, cut] * wide[slot, pl.ds(6 + at, LANES), cut]
            + small_ref[index, 1:2, cut] * wide[slot, pl.ds(7 + at, LANES), cut]
            + small_ref[index, 2:3, cut] * wide[slot, pl.ds(8 + at, LANES), cut]
            + small_ref[3, index:index + 1, cut]
        )

    for chunk in range(2):
        for half in range(2):
            gated_t[chunk, half] = (short(1, half, chunk) * short(2, half, chunk)).T
        pack(chunk, [gated_t[chunk, 0], gated_t[chunk, 1]], send_g)
        exchange(send_g, recv_g, 0, chunk)

    wait_bytes(recv_h.at[pl.ds(0, ctx_n - 1)], h_sem.at[1])
    toeplitz_rows(recv_h, toeplitz, ctx_n)
    for chunk in range(2):
        arrived(recv_g, 0, chunk)
        unpack(chunk, recv_g)
        for chan in range(2):
            for half in range(2):
                blocks[0, pl.ds(STEP + half, 64, stride=2), :] = flat[
                    pl.ds(2 * chan + half, 64, stride=4), :]
            result[...] = channel_conv(
                blocks, phases, shifted, acc, toeplitz, 2 * chunk + chan)
            for half in range(2):
                flat[pl.ds(2 * chan + half, 64, stride=4), :] = result[pl.ds(half, 64, stride=2), :]
        send_y[chunk] = flat[...].reshape(ctx_n, 4, LANES).astype(BF16)
        exchange(send_y, recv_y, 1, chunk)

    for chunk in range(2):
        for half in range(2):
            query_t[chunk, half] = short(0, half, chunk).T

    wait_bytes(w_all.at[pl.ds(0, ch_n - 1)], w_recv)

    @pl.loop(0, ch_n)
    def _(index):
        for chunk in range(2):
            w_t[index, chunk] = w_all[index, cuts[chunk], :].T

    def pass_on(source, chunk, copy_sem, target):
        return remote(oper.at[source, chunk], oper.at[source, chunk], copy_sem,
                      o_recv.at[source, chunk], "ch", target)

    for chunk in range(2):
        skip_t = jnp.broadcast_to(small_ref[4, 0:1, cuts[chunk]], (LANES, LANES)).T
        arrived(recv_y, 1, chunk)
        unpack(chunk, recv_y)
        for half in range(2):
            conv = jnp.concatenate(
                [flat[pl.ds(2 * chan + half, 64, stride=4), :] for chan in range(2)], axis=0)
            oper[my_ch, chunk, :, cuts[half]] = (
                query_t[chunk, half] * (conv + skip_t * gated_t[chunk, half])).astype(BF16)
        for hop in (4, 3, 5, 2, 6, 1, 7):
            pass_on(my_ch, chunk, o_send, lax.rem(my_ch + hop, ch_n)).start()

    bias_t = jnp.broadcast_to(small_ref[4, 1:2, :], (LANES, 256)).T
    total = jnp.concatenate([bias_t, bias_t], axis=1)

    def add(total, source, chunk):
        return total + jnp.dot(w_t[source, chunk], oper[source, chunk], preferred_element_type=F32)

    for chunk in range(2):
        total = add(total, my_ch, chunk)
    for chunk in range(2):
        for hop in (1, 7, 2, 6, 3, 5, 4):
            source = lax.rem(my_ch + hop, ch_n)
            wait_bytes(oper.at[source, chunk], o_recv.at[source, chunk])
            total = add(total, source, chunk)
    out_ref[...] = total.astype(BF16)

    wait_bytes(send_h.at[pl.ds(0, ctx_n - 1)], h_sem.at[0])
    for which, ref in enumerate((send_g, send_y)):
        for chunk in range(2):
            wait_bytes(ref.at[chunk, pl.ds(0, ctx_n - 1)], send_sem.at[which, chunk])
    wait_bytes(w_all.at[pl.ds(0, ch_n - 1)], w_send)
    wait_bytes(oper.at[pl.ds(0, 7)], o_send)


def shards(q, k, v, taps, sbias, filt, skip, weight, obias):
    ctx_n, ch_n = lax.axis_size("ctx"), lax.axis_size("ch")
    vmem = pl.BlockSpec(memory_space=pltpu.VMEM)
    message = pltpu.VMEM((2, ctx_n, 4, LANES), BF16)
    dma = pltpu.SemaphoreType.DMA
    small = jnp.concatenate(
        [taps, sbias[None], jnp.stack([skip, obias, obias])[None]], axis=0)
    return pl.pallas_call(
        functools.partial(kernel, ctx_n, ch_n),
        out_shape=jax.ShapeDtypeStruct((256, 256), BF16),
        in_specs=[pl.BlockSpec(memory_space=pl.ANY)] * 6,
        out_specs=vmem,
        scratch_shapes=[
            pltpu.VMEM((256, 256), BF16),
            pltpu.VMEM((256, 256), BF16),
            pltpu.VMEM((256, 256), BF16),
            pltpu.VMEM((256, 256), F32),
            pltpu.VMEM((5, 3, 256), F32),
            pltpu.VMEM((256, LANES), F32),
            pltpu.VMEM((512, LANES), F32),
            pltpu.VMEM((16, 256), BF16),
            pltpu.VMEM((16, 256), BF16),
            pltpu.VMEM((3, 264, 256), F32),
            pltpu.VMEM((ctx_n, 8, LANES), BF16), message, message,
            pltpu.VMEM((ctx_n, 8, LANES), BF16), message, message,
            pltpu.VMEM((2, 2, LANES, LANES), F32),
            pltpu.VMEM((2, 2, LANES, LANES), F32),
            pltpu.VMEM((4, LANES * PHASE, LANES), BF16),
            pltpu.VMEM((LANES // PHASE, LANES, STEP * PHASE), BF16),
            pltpu.VMEM((LANES // PHASE, STEP + LANES, LANES), F32),
            pltpu.VMEM((LANES // PHASE, STEP + LANES, LANES), F32),
            pltpu.VMEM((LANES, LANES), F32),
            pltpu.VMEM((LANES // PHASE, 8 + LANES, LANES), F32),
            pltpu.VMEM((ch_n, 256, 256), BF16),
            pltpu.VMEM((ch_n, 2, 256, LANES), BF16),
            pltpu.VMEM((ch_n, 2, LANES, 256), BF16),
            dma((2, 2)), dma((2, 2)), dma((2,)), dma, dma, dma, dma((ch_n, 2)), dma((6,)), dma((2,)),
        ],
        compiler_params=pltpu.CompilerParams(
            collective_id=3, has_side_effects=True, vmem_limit_bytes=54 * 2**20 - 256 * 1024),
    )(q, k, v, filt, weight, small)


def solution(mesh):
    return jax.shard_map(
        shards,
        mesh=mesh,
        in_specs=(
            P("ctx", "ch"),
            P("ctx", "ch"),
            P("ctx", "ch"),
            P(None, None, "ch"),
            P(None, "ch"),
            P("ctx", "ch"),
            P("ch"),
            P("ch", None),
            P("ch"),
        ),
        out_specs=P("ch", "ctx"),
        check_vma=False,
    )
```
